32 devices in a mesh: dp: 2 (over x), ctx: 16 (over z, y, core).
Axes of the slice: x: 2, y: 2, z: 4, core: 2. Of those that a mesh axis runs over, the one named last changes fastest.
Arguments:
- grad_output: bfloat16 [2, 2048, 2048], P('dp', 'ctx'), may hold values from -0.125 to 0.125
- conv_input: bfloat16 [2, 2048, 2048], P('dp', 'ctx'), may hold values from -6 to 6
- filter_taps: bfloat16 [2048, 2048], P('ctx'), may hold values from -4 to 4
Outputs:
- grad_input: bfloat16 [2, 2048, 2048], P('dp', 'ctx')
- filter_grad: float32 [2048, 2048], P('ctx', 'dp')
The draws below stay inside these ranges and needn't reach their ends.
All inputs are finite; a program needn't handle non-finite values.
Results may differ from the reference program's by a relative error of at most 0.001.
Values may be sent and summed in bfloat16 or wider, within the bound.
A program may use at most 64 MiB of HBM per device.

```python
import jax
import jax.numpy as jnp

C = 2048
SEQ = 2048
N_DP = 2


def draw_filter_taps(key, part):
    rough_part = jnp.clip(jax.random.normal(key, (SEQ, C), jnp.float32), -4.0, 4.0)
    return rough_part.astype(jnp.bfloat16)


def level_of(own_key, shape, split, least, largest):
    level, own = 1.0, jax.random.fold_in(own_key, 6)
    for dim, shards_of in split:
        heights = jnp.exp(jax.random.uniform(jax.random.fold_in(own, dim), (shards_of,), jnp.float32, least / len(split), largest / len(split)))
        level = level * jnp.repeat(heights, shape[dim] // shards_of).reshape([-1 if axis == dim else 1 for axis in range(len(shape))])
    return level


def normal_values(own_key, extent, deviation, bound, split=(), kind=jnp.bfloat16):
    values = jax.random.normal(own_key, extent, jnp.float32) * deviation
    if len(split) > 0:
        values = level_of(own_key, extent, split, -0.22, 0.18) * values
    return jnp.clip(values, min=-bound, max=bound).astype(kind)


def setup_inputs(seed: int = 0) -> dict:
    arg_keys = jax.random.split(jax.random.key(seed), 4)
    grad_output = normal_values(arg_keys[0], (N_DP, SEQ, C), SEQ ** -0.5, 0.125, ((0, 2), (1, 16)))
    conv_input = normal_values(arg_keys[1], (N_DP, SEQ, C), 1.0, 6.0, ((0, 2), (1, 16)))
    filter_taps = draw_filter_taps(jax.random.fold_in(arg_keys[3], 71), 0)
    return {"grad_output": grad_output, "conv_input": conv_input, "filter_taps": filter_taps}


def reference(grad_output, conv_input, filter_taps):
    length = grad_output.shape[1]
    width = grad_output.shape[2]
    padded = 2 * length
    taps_spectrum = jnp.fft.rfft(filter_taps.astype(jnp.float32), n=padded, axis=0)
    total = jnp.zeros((length, width), jnp.float32)
    grad_parts = []
    for group in range(grad_output.shape[0]):
        grad_spectrum = jnp.fft.rfft(grad_output[group].astype(jnp.float32), n=padded, axis=0)
        input_spectrum = jnp.fft.rfft(conv_input[group].astype(jnp.float32), n=padded, axis=0)
        grad_seq = jnp.fft.irfft(grad_spectrum * jnp.conj(taps_spectrum), n=padded, axis=0)[:length]
        partial_grad = jnp.fft.irfft(grad_spectrum * jnp.conj(input_spectrum), n=padded, axis=0)[:length]
        grad_parts.append(grad_seq.astype(jnp.bfloat16))
        total = total + partial_grad
    return jnp.stack(grad_parts), jnp.transpose(total)
```

```python
import functools
import math

import jax
import jax.numpy as jnp
import numpy as np
from jax import lax
from jax.experimental import pallas as pl
from jax.experimental.pallas import tpu as pltpu
from jax.sharding import PartitionSpec as P


def angle_table(rows, cols, period):
    product = (
        lax.broadcasted_iota(jnp.int32, (rows, cols), 0)
        * lax.broadcasted_iota(jnp.int32, (rows, cols), 1)
        % period
    )
    phase = product.astype(jnp.float32) * (2.0 * math.pi / period)
    return (jnp.cos(phase), jnp.sin(phase))


def forward(values):
    blocks = values.shape[-2]
    tokens = values.shape[-1]
    rows = 2 * blocks
    block_cos, block_sin = angle_table(rows, blocks, rows)
    twist_cos, twist_sin = angle_table(rows, tokens, rows * tokens)
    inner_cos, inner_sin = angle_table(tokens, tokens, tokens)
    block_table = jnp.stack([block_cos, -block_sin])
    first = jnp.einsum("...qj,prq->...prj", values, block_table, precision=lax.Precision.HIGHEST)
    first_re = first[..., 0, :, :]
    first_im = first[..., 1, :, :]
    turned = jnp.stack(
        [first_re * twist_cos + first_im * twist_sin, first_im * twist_cos - first_re * twist_sin],
        axis=-3,
    )
    inner_table = jnp.stack([jnp.stack([inner_cos, -inner_sin]), jnp.stack([inner_sin, inner_cos])])
    return jnp.einsum("...prj,pojm->...orm", turned, inner_table, precision=lax.Precision.HIGHEST)


def inverse(spectrum):
    rows = spectrum.shape[-2]
    tokens = spectrum.shape[-1]
    blocks = rows // 2
    block_cos, block_sin = angle_table(rows, blocks, rows)
    twist_cos, twist_sin = angle_table(rows, tokens, rows * tokens)
    inner_cos, inner_sin = angle_table(tokens, tokens, tokens)
    inner_table = jnp.stack([jnp.stack([inner_cos, inner_sin]), jnp.stack([-inner_sin, inner_cos])])
    back = jnp.einsum("...prm,pomj->...orj", spectrum, inner_table, precision=lax.Precision.HIGHEST)
    back_re = back[..., 0, :, :]
    back_im = back[..., 1, :, :]
    turned = jnp.stack(
        [back_re * twist_cos - back_im * twist_sin, back_im * twist_cos + back_re * twist_sin],
        axis=-3,
    )
    block_table = jnp.stack([block_cos, -block_sin])
    result = jnp.einsum("...prj,prq->...qj", turned, block_table, precision=lax.Precision.HIGHEST)
    return result / (rows * tokens)


def conj_product(left, right):
    left_re = left[:, 0]
    left_im = left[:, 1]
    right_re = right[:, 0]
    right_im = right[:, 1]
    return jnp.stack(
        [left_re * right_re + left_im * right_im, left_im * right_re - left_re * right_im], axis=1
    )


def local(grad_output, conv_input, filter_taps):
    tokens = grad_output.shape[1]
    width = grad_output.shape[2]
    groups = lax.axis_size("ctx")
    group_width = width // groups

    def to_groups(values):
        return jnp.transpose(values.reshape(tokens, groups, group_width), (1, 2, 0))[:, :, None, :]

    grad_cols, input_cols, taps_cols = (
        lax.all_to_all(to_groups(grad_output[0]), "ctx", split_axis=0, concat_axis=2, tiled=True),
        lax.all_to_all(to_groups(conv_input[0]), "ctx", split_axis=0, concat_axis=2, tiled=True),
        lax.all_to_all(to_groups(filter_taps), "ctx", split_axis=0, concat_axis=2, tiled=True),
    )
    filter_spec = forward(taps_cols[0].astype(jnp.float32))
    stacked = jnp.stack([grad_cols[0], input_cols[0]]).astype(jnp.float32)
    spectra = forward(stacked)
    grad_spec = spectra[0]
    input_spec = spectra[1]
    cross = conj_product(grad_spec, filter_spec)
    corr = conj_product(grad_spec, input_spec)
    results = inverse(jnp.stack([cross, corr]))
    grad_cols_out = results[0]
    filter_part = lax.psum_scatter(results[1], "dp", scatter_dimension=1, tiled=True)
    filter_grad = filter_part.reshape(group_width, -1)
    rounded = grad_cols_out.astype(jnp.bfloat16)[None]
    returned = lax.all_to_all(rounded, "ctx", split_axis=2, concat_axis=0, tiled=True)
    grad_input = jnp.transpose(returned[:, :, 0, :], (2, 0, 1)).reshape(tokens, width)[None]
    return (grad_input, filter_grad)


INNER = 256
RADIX = 16
HALF = RADIX // 2
KEPT = HALF + 1
LANES = 128
ROWS = 16
MESH = pl.DeviceIdType.MESH


def inner_tables():
    index = np.arange(INNER)
    phase = 2.0 * np.pi * (np.outer(index, index) % INNER) / INNER
    cos, sin = np.cos(phase), np.sin(phase)
    table = np.block([[cos, sin], [-sin, cos]]).astype(np.float32)
    high = table.astype(jnp.bfloat16)
    low = (table - high.astype(np.float32)).astype(jnp.bfloat16)
    return np.stack([high, low])


def twist_columns():
    phase = 2.0 * np.pi * np.outer(np.arange(INNER), np.arange(1, KEPT)) / (RADIX * INNER)
    columns = np.zeros((INNER, LANES), np.float32)
    columns[:, :HALF] = np.cos(phase)
    columns[:, HALF : 2 * HALF] = np.sin(phase)
    return columns


def cmul(a, c, s):
    return (a[0] * c - a[1] * s, a[0] * s + a[1] * c)


def cadd(a, b):
    return (a[0] + b[0], a[1] + b[1])


def csub(a, b):
    return (a[0] - b[0], a[1] - b[1])


def times_i(a):
    return (-a[1], a[0])


def spread(x):
    s = math.sqrt(0.5)
    a = [x[q] + x[q + 4] for q in range(4)]
    b = [x[q] - x[q + 4] for q in range(4)]
    out = [None] * KEPT
    out[0] = (a[0] + a[2]) + (a[1] + a[3])
    out[8] = (a[0] + a[2]) - (a[1] + a[3])
    out[4] = (a[0] - a[2], a[3] - a[1])
    diff, both = s * (b[1] - b[3]), s * (b[1] + b[3])
    out[2] = (b[0] + diff, -b[2] - both)
    out[6] = (b[0] - diff, b[2] - both)
    u = [(x[0], -x[4])]
    for q in range(1, 4):
        c, t = math.cos(2.0 * math.pi * q / RADIX), math.sin(2.0 * math.pi * q / RADIX)
        u.append((x[q] * c - x[q + 4] * t, -(x[q + 4] * c + x[q] * t)))
    e0, e1 = cadd(u[0], u[2]), csub(u[0], u[2])
    f0, f1 = cadd(u[1], u[3]), times_i(csub(u[1], u[3]))
    out[1] = cadd(e0, f0)
    out[5] = csub(e1, f1)
    v2, v3 = csub(e0, f0), cadd(e1, f1)
    out[7] = (v2[0], -v2[1])
    out[3] = (v3[0], -v3[1])
    return out


def gather(z):
    s = math.sqrt(0.5)
    total, diff = z[0] + z[8], z[0] - z[8]
    plus, minus = total + z[4][0], total - z[4][0]
    sr, si = z[2][0] + z[6][0], z[6][1] - z[2][1]
    p = (s * (z[2][0] - z[2][1]), s * (z[2][0] + z[2][1]))
    w = (-s * (z[6][0] + z[6][1]), s * (z[6][0] - z[6][1]))
    pw, wp = p[0] + w[0], w[1] - p[1]
    down, up = diff - z[4][1], diff + z[4][1]
    even = [plus + sr, down + pw, minus + si, up + wp, plus - sr, down - pw, minus - si, up - wp]
    v = [z[1], z[5], (z[7][0], -z[7][1]), (z[3][0], -z[3][1])]
    e0, e1 = cadd(v[0], v[2]), csub(v[0], v[2])
    f0, f1 = cadd(v[1], v[3]), times_i(csub(v[1], v[3]))
    u = [cadd(e0, f0), cadd(e1, f1), csub(e0, f0), csub(e1, f1)]
    out = [None] * HALF
    for q in range(4):
        o = cmul(u[q], math.cos(2.0 * math.pi * q / RADIX), math.sin(2.0 * math.pi * q / RADIX))
        out[q] = even[q] + o[0]
        out[q + 4] = even[q + 4] - o[1]
    return out


def put_parts(high_ref, low_ref, row, r, value):
    high = value.astype(jnp.bfloat16)
    at = (pl.ds(pl.multiple_of(row, ROWS), ROWS), pl.ds(r * LANES, LANES))
    high_ref[at] = high
    low_ref[at] = (value - high.astype(jnp.float32)).astype(jnp.bfloat16)


def inner_dft(table_ref, high_ref, low_ref, out_ref):
    def block(at):
        high, low = high_ref[:, at], low_ref[:, at]
        out_ref[:, at] = (
            jnp.dot(table_ref[0], high, preferred_element_type=jnp.float32)
            + jnp.dot(table_ref[0], low, preferred_element_type=jnp.float32)
            + jnp.dot(table_ref[1], high, preferred_element_type=jnp.float32)
        )

    @pl.loop(0, HALF // 2)
    def _(i):
        block(pl.ds(pl.multiple_of(i * 2 * LANES, 2 * LANES), 2 * LANES))

    block(pl.ds(HALF * LANES, LANES))


def transform(source_ref, twist_ref, table_ref, high_ref, low_ref, spec_ref):
    @pl.loop(0, INNER // ROWS)
    def _(i):
        row = i * ROWS
        rows = pl.ds(pl.multiple_of(row, ROWS), ROWS)
        x = [
            source_ref[pl.ds(pl.multiple_of(q * INNER + row, ROWS), ROWS), :].astype(jnp.float32)
            for q in range(HALF)
        ]
        out = spread(x)
        put_parts(high_ref, low_ref, row, 0, out[0])
        put_parts(high_ref, low_ref, INNER + row, 0, jnp.zeros_like(out[0]))
        out[8] = (out[8], None)
        for r in range(1, KEPT):
            c, s = twist_ref[r - 1, rows, :], twist_ref[HALF + r - 1, rows, :]
            re, im = out[r]
            if im is None:
                re, im = re * c, -(re * s)
            else:
                re, im = re * c + im * s, im * c - re * s
            put_parts(high_ref, low_ref, row, r, re)
            put_parts(high_ref, low_ref, INNER + row, r, im)

    inner_dft(table_ref, high_ref, low_ref, spec_ref)


def correlate(left_ref, right_ref, twist_ref, table_ref, high_ref, low_ref, work_ref, store):
    @pl.loop(0, INNER // ROWS)
    def _(i):
        row = i * ROWS
        top = pl.ds(pl.multiple_of(row, ROWS), ROWS)
        bottom = pl.ds(pl.multiple_of(INNER + row, ROWS), ROWS)
        for r in range(KEPT):
            lanes = pl.ds(r * LANES, LANES)
            scale = (1.0 if r in (0, HALF) else 2.0) / (RADIX * INNER)
            lr, li = left_ref[top, lanes] * scale, left_ref[bottom, lanes] * scale
            rr, ri = right_ref[top, lanes], right_ref[bottom, lanes]
            put_parts(high_ref, low_ref, row, r, li * rr - lr * ri)
            put_parts(high_ref, low_ref, INNER + row, r, lr * rr + li * ri)

    inner_dft(table_ref, high_ref, low_ref, work_ref)

    @pl.loop(0, INNER // ROWS)
    def _(i):
        row = i * ROWS
        top = pl.ds(pl.multiple_of(row, ROWS), ROWS)
        bottom = pl.ds(pl.multiple_of(INNER + row, ROWS), ROWS)
        z = [work_ref[bottom, pl.ds(0, LANES)]]
        for r in range(1, KEPT):
            lanes = pl.ds(r * LANES, LANES)
            im, re = work_ref[top, lanes], work_ref[bottom, lanes]
            c, s = twist_ref[r - 1, top, :], twist_ref[HALF + r - 1, top, :]
            z.append((re * c - im * s, re * s + im * c))
        z[8] = z[8][0]
        for q, value in enumerate(gather(z)):
            store(q * INNER + row, value)


def kernel(
    groups,
    grad_ref,
    input_ref,
    taps_ref,
    table_ref,
    columns_ref,
    grad_input_ref,
    filter_grad_ref,
    grad_in,
    taps_in,
    input_in,
    grad_spec,
    taps_spec,
    input_spec,
    work,
    high,
    low,
    twist,
    back,
    partial,
    arrived,
    send_sem,
    recv_sem,
    own_sem,
    pair_send,
    pair_recv,
):
    tokens = grad_ref.shape[0]
    half = partial.shape[0] // 2
    me = lax.axis_index("ctx")
    group = lax.axis_index("dp")
    other = 1 - group

    barrier = pltpu.get_barrier_semaphore()

    @pl.loop(1, groups)
    def _(d):
        pl.semaphore_signal(
            barrier, inc=1, device_id=(group, lax.rem(me + d, groups)), device_id_type=MESH
        )

    pl.semaphore_signal(barrier, inc=1, device_id=(other, me), device_id_type=MESH)
    pl.semaphore_wait(barrier, groups)

    def rows_of(device):
        return pl.ds(pl.multiple_of(device * tokens, tokens), tokens)

    def lanes_of(device):
        return pl.ds(pl.multiple_of(device * LANES, LANES), LANES)

    outward = ((grad_ref, grad_in), (taps_ref, taps_in), (input_ref, input_in))

    def copy_out(a, peer, dest_rows, recv_at):
        source, landing = outward[a]
        return pltpu.make_async_remote_copy(
            src_ref=source.at[:, lanes_of(peer)],
            dst_ref=landing.at[rows_of(dest_rows), :],
            send_sem=send_sem.at[a, peer],
            recv_sem=recv_sem.at[a, recv_at],
            device_id=(group, peer),
            device_id_type=MESH,
        )

    def copy_back(peer, dest_lanes, recv_at):
        return pltpu.make_async_remote_copy(
            src_ref=back.at[rows_of(peer), :],
            dst_ref=grad_input_ref.at[:, lanes_of(dest_lanes)],
            send_sem=send_sem.at[3, peer],
            recv_sem=recv_sem.at[3, recv_at],
            device_id=(group, peer),
            device_id_type=MESH,
        )

    def own_out(a):
        source, landing = outward[a]
        return pltpu.make_async_copy(
            source.at[:, lanes_of(me)], landing.at[rows_of(me), :], own_sem.at[a]
        )

    def own_back():
        return pltpu.make_async_copy(
            back.at[rows_of(me), :], grad_input_ref.at[:, lanes_of(me)], own_sem.at[3]
        )

    for a in range(3):

        @pl.loop(1, groups)
        def _(d):
            copy_out(a, lax.rem(me + d, groups), me, me).start()

        own_out(a).start()

    for i in range(2 * HALF):
        twist[i] = jnp.broadcast_to(columns_ref[:, i : i + 1], (INNER, LANES))

    def wait_for(a):
        own_out(a).wait()

        @pl.loop(1, groups)
        def _(d):
            peer = lax.rem(me + d, groups)
            copy_out(a, peer, peer, peer).wait_recv()

    shared = (twist, table_ref, high, low)
    wait_for(0)
    transform(grad_in, *shared, grad_spec)
    wait_for(1)
    transform(taps_in, *shared, taps_spec)

    def store_back(row, value):
        back[pl.ds(pl.multiple_of(row, ROWS), ROWS), :] = value.astype(jnp.bfloat16)

    correlate(grad_spec, taps_spec, *shared, work, store_back)

    @pl.loop(1, groups)
    def _(d):
        copy_back(lax.rem(me + d, groups), me, me).start()

    own_back().start()
    wait_for(2)
    transform(input_in, *shared, input_spec)

    def store_partial(row, value):
        partial[pl.ds(pl.multiple_of(row, ROWS), ROWS), :] = value

    correlate(grad_spec, input_spec, *shared, work, store_partial)
    pair = pltpu.make_async_remote_copy(
        src_ref=partial.at[pl.ds(pl.multiple_of(other * half, half), half), :],
        dst_ref=arrived,
        send_sem=pair_send,
        recv_sem=pair_recv,
        device_id=(other, me),
        device_id_type=MESH,
    )
    pair.start()
    pair.wait()

    for i in range(half // LANES):
        mine = partial[pl.ds(pl.multiple_of(group * half + i * LANES, LANES), LANES), :]
        filter_grad_ref[:, i * LANES : (i + 1) * LANES] = jnp.transpose(
            mine + arrived[i * LANES : (i + 1) * LANES, :]
        )

    own_back().wait()

    @pl.loop(1, groups)
    def _(d):
        peer = lax.rem(me + d, groups)
        copy_back(peer, peer, peer).wait()
        for a in range(3):
            copy_out(a, peer, peer, peer).wait_send()


def fused(grad_output, conv_input, filter_taps):
    groups = lax.axis_size("ctx")
    tokens, width = filter_taps.shape
    length = groups * tokens
    anywhere = pl.BlockSpec(memory_space=pl.ANY)
    vmem = pl.BlockSpec(memory_space=pltpu.VMEM)
    landing = pltpu.VMEM((length, LANES), jnp.bfloat16)
    spec = pltpu.VMEM((2 * INNER, KEPT * LANES), jnp.float32)
    part = pltpu.VMEM((2 * INNER, KEPT * LANES), jnp.bfloat16)
    grad_input, filter_grad = pl.pallas_call(
        functools.partial(kernel, groups),
        out_shape=(
            jax.ShapeDtypeStruct((tokens, width), jnp.bfloat16),
            jax.ShapeDtypeStruct((LANES, length // 2), jnp.float32),
        ),
        in_specs=[anywhere, anywhere, anywhere, vmem, vmem],
        out_specs=(anywhere, vmem),
        scratch_shapes=[
            landing,
            landing,
            landing,
            spec,
            spec,
            spec,
            spec,
            part,
            part,
            pltpu.VMEM((2 * HALF, INNER, LANES), jnp.float32),
            pltpu.VMEM((length, LANES), jnp.bfloat16),
            pltpu.VMEM((length, LANES), jnp.float32),
            pltpu.VMEM((length // 2, LANES), jnp.float32),
            pltpu.SemaphoreType.DMA((4, groups)),
            pltpu.SemaphoreType.DMA((4, groups)),
            pltpu.SemaphoreType.DMA((4,)),
            pltpu.SemaphoreType.DMA,
            pltpu.SemaphoreType.DMA,
        ],
        compiler_params=pltpu.CompilerParams(
            collective_id=0, has_side_effects=True, vmem_limit_bytes=40 * 1024 * 1024
        ),
        cost_estimate=pl.CostEstimate(
            flops=5 * 3 * 2 * 512 * 512 * KEPT * LANES, bytes_accessed=6 << 20, transcendentals=0
        ),
    )(
        grad_output[0],
        conv_input[0],
        filter_taps,
        jnp.asarray(inner_tables()),
        jnp.asarray(twist_columns()),
    )
    return (grad_input[None], filter_grad)


def any_size(grad_output, conv_input, filter_taps):
    groups = lax.axis_size("ctx")
    tokens, width = filter_taps.shape
    fits = (
        lax.axis_size("dp") == 2
        and groups * tokens == HALF * INNER
        and width == groups * LANES
        and tokens % ROWS == 0
    )
    return (fused if fits else local)(grad_output, conv_input, filter_taps)


def solution(mesh):
    placed = (P("dp", "ctx", None), P("dp", "ctx", None), P("ctx", None))
    return jax.shard_map(
        any_size,
        mesh=mesh,
        in_specs=placed,
        out_specs=(P("dp", "ctx", None), P("ctx", "dp")),
        check_vma=False,
    )
```

```python
import functools
import math

import jax
import jax.numpy as jnp
import numpy as np
from jax import lax
from jax.experimental import pallas as pl
from jax.experimental.pallas import tpu as pltpu
from jax.sharding import PartitionSpec as P


def angle_table(rows, cols, period):
    product = (
        lax.broadcasted_iota(jnp.int32, (rows, cols), 0)
        * lax.broadcasted_iota(jnp.int32, (rows, cols), 1)
        % period
    )
    phase = product.astype(jnp.float32) * (2.0 * math.pi / period)
    return (jnp.cos(phase), jnp.sin(phase))


def forward(values):
    blocks = values.shape[-2]
    tokens = values.shape[-1]
    rows = 2 * blocks
    block_cos, block_sin = angle_table(rows, blocks, rows)
    twist_cos, twist_sin = angle_table(rows, tokens, rows * tokens)
    inner_cos, inner_sin = angle_table(tokens, tokens, tokens)
    block_table = jnp.stack([block_cos, -block_sin])
    first = jnp.einsum("...qj,prq->...prj", values, block_table, precision=lax.Precision.HIGHEST)
    first_re = first[..., 0, :, :]
    first_im = first[..., 1, :, :]
    turned = jnp.stack(
        [first_re * twist_cos + first_im * twist_sin, first_im * twist_cos - first_re * twist_sin],
        axis=-3,
    )
    inner_table = jnp.stack([jnp.stack([inner_cos, -inner_sin]), jnp.stack([inner_sin, inner_cos])])
    return jnp.einsum("...prj,pojm->...orm", turned, inner_table, precision=lax.Precision.HIGHEST)


def inverse(spectrum):
    rows = spectrum.shape[-2]
    tokens = spectrum.shape[-1]
    blocks = rows // 2
    block_cos, block_sin = angle_table(rows, blocks, rows)
    twist_cos, twist_sin = angle_table(rows, tokens, rows * tokens)
    inner_cos, inner_sin = angle_table(tokens, tokens, tokens)
    inner_table = jnp.stack([jnp.stack([inner_cos, inner_sin]), jnp.stack([-inner_sin, inner_cos])])
    back = jnp.einsum("...prm,pomj->...orj", spectrum, inner_table, precision=lax.Precision.HIGHEST)
    back_re = back[..., 0, :, :]
    back_im = back[..., 1, :, :]
    turned = jnp.stack(
        [back_re * twist_cos - back_im * twist_sin, back_im * twist_cos + back_re * twist_sin],
        axis=-3,
    )
    block_table = jnp.stack([block_cos, -block_sin])
    result = jnp.einsum("...prj,prq->...qj", turned, block_table, precision=lax.Precision.HIGHEST)
    return result / (rows * tokens)


def conj_product(left, right):
    left_re = left[:, 0]
    left_im = left[:, 1]
    right_re = right[:, 0]
    right_im = right[:, 1]
    return jnp.stack(
        [left_re * right_re + left_im * right_im, left_im * right_re - left_re * right_im], axis=1
    )


def local(grad_output, conv_input, filter_taps):
    tokens = grad_output.shape[1]
    width = grad_output.shape[2]
    groups = lax.axis_size("ctx")
    group_width = width // groups

    def to_groups(values):
        return jnp.transpose(values.reshape(tokens, groups, group_width), (1, 2, 0))[:, :, None, :]

    grad_cols, input_cols, taps_cols = (
        lax.all_to_all(to_groups(grad_output[0]), "ctx", split_axis=0, concat_axis=2, tiled=True),
        lax.all_to_all(to_groups(conv_input[0]), "ctx", split_axis=0, concat_axis=2, tiled=True),
        lax.all_to_all(to_groups(filter_taps), "ctx", split_axis=0, concat_axis=2, tiled=True),
    )
    filter_spec = forward(taps_cols[0].astype(jnp.float32))
    stacked = jnp.stack([grad_cols[0], input_cols[0]]).astype(jnp.float32)
    spectra = forward(stacked)
    grad_spec = spectra[0]
    input_spec = spectra[1]
    cross = conj_product(grad_spec, filter_spec)
    corr = conj_product(grad_spec, input_spec)
    results = inverse(jnp.stack([cross, corr]))
    grad_cols_out = results[0]
    filter_part = lax.psum_scatter(results[1], "dp", scatter_dimension=1, tiled=True)
    filter_grad = filter_part.reshape(group_width, -1)
    rounded = grad_cols_out.astype(jnp.bfloat16)[None]
    returned = lax.all_to_all(rounded, "ctx", split_axis=2, concat_axis=0, tiled=True)
    grad_input = jnp.transpose(returned[:, :, 0, :], (2, 0, 1)).reshape(tokens, width)[None]
    return (grad_input, filter_grad)


INNER = 256
RADIX = 16
HALF = RADIX // 2
KEPT = HALF + 1
LANES = 128
ROWS = 16
MESH = pl.DeviceIdType.MESH


def inner_tables():
    index = np.arange(INNER)
    phase = 2.0 * np.pi * (np.outer(index, index) % INNER) / INNER
    cos, sin = np.cos(phase), np.sin(phase)
    table = np.block([[cos, sin], [-sin, cos]]).astype(np.float32)
    high = table.astype(jnp.bfloat16)
    low = (table - high.astype(np.float32)).astype(jnp.bfloat16)
    return np.stack([high, low])


def twist_columns():
    phase = 2.0 * np.pi * np.outer(np.arange(INNER), np.arange(1, KEPT)) / (RADIX * INNER)
    columns = np.zeros((INNER, LANES), np.float32)
    columns[:, :HALF] = np.cos(phase)
    columns[:, HALF : 2 * HALF] = np.sin(phase)
    return columns


def cmul(a, c, s):
    return (a[0] * c - a[1] * s, a[0] * s + a[1] * c)


def cadd(a, b):
    return (a[0] + b[0], a[1] + b[1])


def csub(a, b):
    return (a[0] - b[0], a[1] - b[1])


def times_i(a):
    return (-a[1], a[0])


def spread(x):
    s = math.sqrt(0.5)
    a = [x[q] + x[q + 4] for q in range(4)]
    b = [x[q] - x[q + 4] for q in range(4)]
    out = [None] * KEPT
    out[0] = (a[0] + a[2]) + (a[1] + a[3])
    out[8] = (a[0] + a[2]) - (a[1] + a[3])
    out[4] = (a[0] - a[2], a[3] - a[1])
    diff, both = s * (b[1] - b[3]), s * (b[1] + b[3])
    out[2] = (b[0] + diff, -b[2] - both)
    out[6] = (b[0] - diff, b[2] - both)
    u = [(x[0], -x[4])]
    for q in range(1, 4):
        c, t = math.cos(2.0 * math.pi * q / RADIX), math.sin(2.0 * math.pi * q / RADIX)
        u.append((x[q] * c - x[q + 4] * t, -(x[q + 4] * c + x[q] * t)))
    e0, e1 = cadd(u[0], u[2]), csub(u[0], u[2])
    f0, f1 = cadd(u[1], u[3]), times_i(csub(u[1], u[3]))
    out[1] = cadd(e0, f0)
    out[5] = csub(e1, f1)
    v2, v3 = csub(e0, f0), cadd(e1, f1)
    out[7] = (v2[0], -v2[1])
    out[3] = (v3[0], -v3[1])
    return out


def gather(z):
    s = math.sqrt(0.5)
    total, diff = z[0] + z[8], z[0] - z[8]
    plus, minus = total + z[4][0], total - z[4][0]
    sr, si = z[2][0] + z[6][0], z[6][1] - z[2][1]
    p = (s * (z[2][0] - z[2][1]), s * (z[2][0] + z[2][1]))
    w = (-s * (z[6][0] + z[6][1]), s * (z[6][0] - z[6][1]))
    pw, wp = p[0] + w[0], w[1] - p[1]
    down, up = diff - z[4][1], diff + z[4][1]
    even = [plus + sr, down + pw, minus + si, up + wp, plus - sr, down - pw, minus - si, up - wp]
    v = [z[1], z[5], (z[7][0], -z[7][1]), (z[3][0], -z[3][1])]
    e0, e1 = cadd(v[0], v[2]), csub(v[0], v[2])
    f0, f1 = cadd(v[1], v[3]), times_i(csub(v[1], v[3]))
    u = [cadd(e0, f0), cadd(e1, f1), csub(e0, f0), csub(e1, f1)]
    out = [None] * HALF
    for q in range(4):
        o = cmul(u[q], math.cos(2.0 * math.pi * q / RADIX), math.sin(2.0 * math.pi * q / RADIX))
        out[q] = even[q] + o[0]
        out[q + 4] = even[q + 4] - o[1]
    return out


def put_parts(high_ref, low_ref, row, r, value):
    high = value.astype(jnp.bfloat16)
    at = (pl.ds(pl.multiple_of(row, ROWS), ROWS), pl.ds(r * LANES, LANES))
    high_ref[at] = high
    low_ref[at] = (value - high.astype(jnp.float32)).astype(jnp.bfloat16)


def inner_dft(table_ref, high_ref, low_ref, out_ref):
    def block(at):
        high, low = high_ref[:, at], low_ref[:, at]
        out_ref[:, at] = (
            jnp.dot(table_ref[0], high, preferred_element_type=jnp.float32)
            + jnp.dot(table_ref[0], low, preferred_element_type=jnp.float32)
            + jnp.dot(table_ref[1], high, preferred_element_type=jnp.float32)
        )

    @pl.loop(0, HALF // 2)
    def _(i):
        block(pl.ds(pl.multiple_of(i * 2 * LANES, 2 * LANES), 2 * LANES))

    block(pl.ds(HALF * LANES, LANES))


def transform(source_ref, twist_ref, table_ref, high_ref, low_ref, spec_ref):
    @pl.loop(0, INNER // ROWS)
    def _(i):
        row = i * ROWS
        rows = pl.ds(pl.multiple_of(row, ROWS), ROWS)
        x = [
            source_ref[pl.ds(pl.multiple_of(q * INNER + row, ROWS), ROWS), :].astype(jnp.float32)
            for q in range(HALF)
        ]
        out = spread(x)
        put_parts(high_ref, low_ref, row, 0, out[0])
        put_parts(high_ref, low_ref, INNER + row, 0, jnp.zeros_like(out[0]))
        out[8] = (out[8], None)
        for r in range(1, KEPT):
            c, s = twist_ref[r - 1, rows, :], twist_ref[HALF + r - 1, rows, :]
            re, im = out[r]
            if im is None:
                re, im = re * c, -(re * s)
            else:
                re, im = re * c + im * s, im * c - re * s
            put_parts(high_ref, low_ref, row, r, re)
            put_parts(high_ref, low_ref, INNER + row, r, im)

    inner_dft(table_ref, high_ref, low_ref, spec_ref)


def correlate(left_ref, right_ref, twist_ref, table_ref, high_ref, low_ref, work_ref, store, flush):
    @pl.loop(0, INNER // ROWS)
    def _(i):
        row = i * ROWS
        top = pl.ds(pl.multiple_of(row, ROWS), ROWS)
        bottom = pl.ds(pl.multiple_of(INNER + row, ROWS), ROWS)
        for r in range(KEPT):
            lanes = pl.ds(r * LANES, LANES)
            scale = (1.0 if r in (0, HALF) else 2.0) / (RADIX * INNER)
            lr, li = left_ref[top, lanes] * scale, left_ref[bottom, lanes] * scale
            rr, ri = right_ref[top, lanes], right_ref[bottom, lanes]
            put_parts(high_ref, low_ref, row, r, li * rr - lr * ri)
            put_parts(high_ref, low_ref, INNER + row, r, lr * rr + li * ri)

    inner_dft(table_ref, high_ref, low_ref, work_ref)

    def finish(i):
        row = i * ROWS
        top = pl.ds(pl.multiple_of(row, ROWS), ROWS)
        bottom = pl.ds(pl.multiple_of(INNER + row, ROWS), ROWS)
        z = [work_ref[bottom, pl.ds(0, LANES)]]
        for r in range(1, KEPT):
            lanes = pl.ds(r * LANES, LANES)
            im, re = work_ref[top, lanes], work_ref[bottom, lanes]
            c, s = twist_ref[r - 1, top, :], twist_ref[HALF + r - 1, top, :]
            z.append((re * c - im * s, re * s + im * c))
        z[8] = z[8][0]
        for q, value in enumerate(gather(z)):
            store(q * INNER + row, value)

    steps = INNER // ROWS // 2
    pl.loop(0, steps)(finish)
    flush(0)
    pl.loop(steps, 2 * steps)(finish)
    flush(1)


def kernel(
    groups,
    grad_ref,
    input_ref,
    taps_ref,
    table_hbm,
    columns_hbm,
    grad_input_ref,
    filter_grad_ref,
    grad_in,
    taps_in,
    input_in,
    grad_spec,
    taps_spec,
    input_spec,
    work,
    high,
    low,
    twist,
    back,
    partial,
    arrived,
    table_ref,
    columns_ref,
    table_sem,
    send_sem,
    recv_sem,
    own_sem,
    pair_send,
    pair_recv,
):
    tokens = grad_ref.shape[0]
    half = partial.shape[0] // 2
    me = lax.axis_index("ctx")
    group = lax.axis_index("dp")
    other = 1 - group

    table_copy = pltpu.make_async_copy(table_hbm, table_ref, table_sem.at[0])
    columns_copy = pltpu.make_async_copy(columns_hbm, columns_ref, table_sem.at[1])
    columns_copy.start()
    table_copy.start()

    barrier = pltpu.get_barrier_semaphore()

    @pl.loop(1, groups)
    def _(d):
        pl.semaphore_signal(
            barrier, inc=1, device_id=(group, lax.rem(me + d, groups)), device_id_type=MESH
        )

    pl.semaphore_signal(barrier, inc=1, device_id=(other, me), device_id_type=MESH)
    pl.semaphore_wait(barrier, groups)

    def rows_of(device):
        return pl.ds(pl.multiple_of(device * tokens, tokens), tokens)

    def lanes_of(device):
        return pl.ds(pl.multiple_of(device * LANES, LANES), LANES)

    outward = ((grad_ref, grad_in), (input_ref, input_in), (taps_ref, taps_in))

    def copy_out(a, peer, dest_rows, recv_at):
        source, landing = outward[a]
        return pltpu.make_async_remote_copy(
            src_ref=source.at[:, lanes_of(peer)],
            dst_ref=landing.at[rows_of(dest_rows), :],
            send_sem=send_sem.at[a, peer],
            recv_sem=recv_sem.at[a, recv_at],
            device_id=(group, peer),
            device_id_type=MESH,
        )

    def copy_back(peer, dest_lanes, recv_at):
        return pltpu.make_async_remote_copy(
            src_ref=back.at[rows_of(peer), :],
            dst_ref=grad_input_ref.at[:, lanes_of(dest_lanes)],
            send_sem=send_sem.at[3, peer],
            recv_sem=recv_sem.at[3, recv_at],
            device_id=(group, peer),
            device_id_type=MESH,
        )

    def own_out(a):
        source, landing = outward[a]
        return pltpu.make_async_copy(
            source.at[:, lanes_of(me)], landing.at[rows_of(me), :], own_sem.at[a]
        )

    def own_back():
        return pltpu.make_async_copy(
            back.at[rows_of(me), :], grad_input_ref.at[:, lanes_of(me)], own_sem.at[3]
        )

    for a in range(3):

        @pl.loop(1, groups)
        def _(d):
            copy_out(a, lax.rem(me + d, groups), me, me).start()

        own_out(a).start()

    columns_copy.wait()
    for i in range(2 * HALF):
        twist[i] = jnp.broadcast_to(columns_ref[:, i : i + 1], (INNER, LANES))
    table_copy.wait()

    def wait_for(a):
        own_out(a).wait()

        @pl.loop(1, groups)
        def _(d):
            peer = lax.rem(me + d, groups)
            copy_out(a, peer, peer, peer).wait_recv()

    shared = (twist, table_ref, high, low)
    wait_for(0)
    transform(grad_in, *shared, grad_spec)
    wait_for(1)
    transform(input_in, *shared, input_spec)

    def store_partial(row, value):
        partial[pl.ds(pl.multiple_of(row, ROWS), ROWS), :] = value

    def pair_copy(part, q):
        rows = INNER // 2
        at = q * INNER + part * rows
        return pltpu.make_async_remote_copy(
            src_ref=partial.at[pl.ds(pl.multiple_of(other * half + at, rows), rows), :],
            dst_ref=arrived.at[pl.ds(at, rows), :],
            send_sem=pair_send.at[part, q],
            recv_sem=pair_recv.at[part, q],
            device_id=(other, me),
            device_id_type=MESH,
        )

    def flush_partial(part):
        for q in range(HALF // 2):
            pair_copy(part, q).start()

    correlate(grad_spec, input_spec, *shared, work, store_partial, flush_partial)
    wait_for(2)
    transform(taps_in, *shared, taps_spec)

    def store_back(row, value):
        back[pl.ds(pl.multiple_of(row, ROWS), ROWS), :] = value.astype(jnp.bfloat16)

    def flush_back(part):
        @pl.loop(0, groups // 2)
        def _(d):
            peer = lax.rem(me + 2 * d, groups) // 2 * 2 + part

            @pl.when(peer != me)
            def _():
                copy_back(peer, me, me).start()

            @pl.when(peer == me)
            def _():
                own_back().start()

    correlate(grad_spec, taps_spec, *shared, work, store_back, flush_back)

    for part in range(2):
        for q in range(HALF // 2):
            pair_copy(part, q).wait()

    for i in range(half // LANES):
        mine = partial[pl.ds(pl.multiple_of(group * half + i * LANES, LANES), LANES), :]
        filter_grad_ref[:, i * LANES : (i + 1) * LANES] = jnp.transpose(
            mine + arrived[i * LANES : (i + 1) * LANES, :]
        )

    own_back().wait()

    @pl.loop(1, groups)
    def _(d):
        peer = lax.rem(me + d, groups)
        copy_back(peer, peer, peer).wait()
        for a in range(3):
            copy_out(a, peer, peer, peer).wait_send()


def fused(grad_output, conv_input, filter_taps):
    groups = lax.axis_size("ctx")
    tokens, width = filter_taps.shape
    length = groups * tokens
    anywhere = pl.BlockSpec(memory_space=pl.ANY)
    vmem = pl.BlockSpec(memory_space=pltpu.VMEM)
    landing = pltpu.VMEM((length, LANES), jnp.bfloat16)
    spec = pltpu.VMEM((2 * INNER, KEPT * LANES), jnp.float32)
    part = pltpu.VMEM((2 * INNER, KEPT * LANES), jnp.bfloat16)
    grad_input, filter_grad = pl.pallas_call(
        functools.partial(kernel, groups),
        out_shape=(
            jax.ShapeDtypeStruct((tokens, width), jnp.bfloat16),
            jax.ShapeDtypeStruct((LANES, length // 2), jnp.float32),
        ),
        in_specs=[anywhere] * 5,
        out_specs=(anywhere, vmem),
        scratch_shapes=[
            landing,
            landing,
            landing,
            spec,
            spec,
            spec,
            spec,
            part,
            part,
            pltpu.VMEM((2 * HALF, INNER, LANES), jnp.float32),
            pltpu.VMEM((length, LANES), jnp.bfloat16),
            pltpu.VMEM((length, LANES), jnp.float32),
            pltpu.VMEM((length // 2, LANES), jnp.float32),
            pltpu.VMEM((2, 2 * INNER, 2 * INNER), jnp.bfloat16),
            pltpu.VMEM((INNER, LANES), jnp.float32),
            pltpu.SemaphoreType.DMA((2,)),
            pltpu.SemaphoreType.DMA((4, groups)),
            pltpu.SemaphoreType.DMA((4, groups)),
            pltpu.SemaphoreType.DMA((4,)),
            pltpu.SemaphoreType.DMA((2, HALF // 2)),
            pltpu.SemaphoreType.DMA((2, HALF // 2)),
        ],
        compiler_params=pltpu.CompilerParams(
            collective_id=0, has_side_effects=True, vmem_limit_bytes=63 * 1024 * 1024
        ),
        cost_estimate=pl.CostEstimate(
            flops=5 * 3 * 2 * 512 * 512 * KEPT * LANES, bytes_accessed=6 << 20, transcendentals=0
        ),
    )(
        grad_output[0],
        conv_input[0],
        filter_taps,
        jnp.asarray(inner_tables()),
        jnp.asarray(twist_columns()),
    )
    return (grad_input[None], filter_grad)


def any_size(grad_output, conv_input, filter_taps):
    groups = lax.axis_size("ctx")
    tokens, width = filter_taps.shape
    fits = (
        lax.axis_size("dp") == 2
        and groups * tokens == HALF * INNER
        and width == groups * LANES
        and 2 * tokens == INNER
    )
    return (fused if fits else local)(grad_output, conv_input, filter_taps)


def solution(mesh):
    placed = (P("dp", "ctx", None), P("dp", "ctx", None), P("ctx", None))
    return jax.shard_map(
        any_size,
        mesh=mesh,
        in_specs=placed,
        out_specs=(P("dp", "ctx", None), P("ctx", "dp")),
        check_vma=False,
    )
```

```python
import functools
import math

import jax
import jax.numpy as jnp
import numpy as np
from jax import lax
from jax.experimental import pallas as pl
from jax.experimental.pallas import tpu as pltpu
from jax.sharding import PartitionSpec as P


def angle_table(rows, cols, period):
    product = (
        lax.broadcasted_iota(jnp.int32, (rows, cols), 0)
        * lax.broadcasted_iota(jnp.int32, (rows, cols), 1)
        % period
    )
    phase = product.astype(jnp.float32) * (2.0 * math.pi / period)
    return (jnp.cos(phase), jnp.sin(phase))


def forward(values):
    blocks = values.shape[-2]
    tokens = values.shape[-1]
    rows = 2 * blocks
    block_cos, block_sin = angle_table(rows, blocks, rows)
    twist_cos, twist_sin = angle_table(rows, tokens, rows * tokens)
    inner_cos, inner_sin = angle_table(tokens, tokens, tokens)
    block_table = jnp.stack([block_cos, -block_sin])
    first = jnp.einsum("...qj,prq->...prj", values, block_table, precision=lax.Precision.HIGHEST)
    first_re = first[..., 0, :, :]
    first_im = first[..., 1, :, :]
    turned = jnp.stack(
        [first_re * twist_cos + first_im * twist_sin, first_im * twist_cos - first_re * twist_sin],
        axis=-3,
    )
    inner_table = jnp.stack([jnp.stack([inner_cos, -inner_sin]), jnp.stack([inner_sin, inner_cos])])
    return jnp.einsum("...prj,pojm->...orm", turned, inner_table, precision=lax.Precision.HIGHEST)


def inverse(spectrum):
    rows = spectrum.shape[-2]
    tokens = spectrum.shape[-1]
    blocks = rows // 2
    block_cos, block_sin = angle_table(rows, blocks, rows)
    twist_cos, twist_sin = angle_table(rows, tokens, rows * tokens)
    inner_cos, inner_sin = angle_table(tokens, tokens, tokens)
    inner_table = jnp.stack([jnp.stack([inner_cos, inner_sin]), jnp.stack([-inner_sin, inner_cos])])
    back = jnp.einsum("...prm,pomj->...orj", spectrum, inner_table, precision=lax.Precision.HIGHEST)
    back_re = back[..., 0, :, :]
    back_im = back[..., 1, :, :]
    turned = jnp.stack(
        [back_re * twist_cos - back_im * twist_sin, back_im * twist_cos + back_re * twist_sin],
        axis=-3,
    )
    block_table = jnp.stack([block_cos, -block_sin])
    result = jnp.einsum("...prj,prq->...qj", turned, block_table, precision=lax.Precision.HIGHEST)
    return result / (rows * tokens)


def conj_product(left, right):
    left_re = left[:, 0]
    left_im = left[:, 1]
    right_re = right[:, 0]
    right_im = right[:, 1]
    return jnp.stack(
        [left_re * right_re + left_im * right_im, left_im * right_re - left_re * right_im], axis=1
    )


def local(grad_output, conv_input, filter_taps):
    tokens = grad_output.shape[1]
    width = grad_output.shape[2]
    groups = lax.axis_size("ctx")
    group_width = width // groups

    def to_groups(values):
        return jnp.transpose(values.reshape(tokens, groups, group_width), (1, 2, 0))[:, :, None, :]

    grad_cols, input_cols, taps_cols = (
        lax.all_to_all(to_groups(grad_output[0]), "ctx", split_axis=0, concat_axis=2, tiled=True),
        lax.all_to_all(to_groups(conv_input[0]), "ctx", split_axis=0, concat_axis=2, tiled=True),
        lax.all_to_all(to_groups(filter_taps), "ctx", split_axis=0, concat_axis=2, tiled=True),
    )
    filter_spec = forward(taps_cols[0].astype(jnp.float32))
    stacked = jnp.stack([grad_cols[0], input_cols[0]]).astype(jnp.float32)
    spectra = forward(stacked)
    grad_spec = spectra[0]
    input_spec = spectra[1]
    cross = conj_product(grad_spec, filter_spec)
    corr = conj_product(grad_spec, input_spec)
    results = inverse(jnp.stack([cross, corr]))
    grad_cols_out = results[0]
    filter_part = lax.psum_scatter(results[1], "dp", scatter_dimension=1, tiled=True)
    filter_grad = filter_part.reshape(group_width, -1)
    rounded = grad_cols_out.astype(jnp.bfloat16)[None]
    returned = lax.all_to_all(rounded, "ctx", split_axis=2, concat_axis=0, tiled=True)
    grad_input = jnp.transpose(returned[:, :, 0, :], (2, 0, 1)).reshape(tokens, width)[None]
    return (grad_input, filter_grad)


INNER = 256
RADIX = 16
HALF = RADIX // 2
KEPT = HALF + 1
LANES = 128
ROWS = 16
MESH = pl.DeviceIdType.MESH


def inner_tables():
    index = np.arange(INNER)
    phase = 2.0 * np.pi * (np.outer(index, index) % INNER) / INNER
    cos, sin = np.cos(phase), np.sin(phase)
    table = np.block([[cos, sin], [-sin, cos]]).astype(np.float32)
    high = table.astype(jnp.bfloat16)
    low = (table - high.astype(np.float32)).astype(jnp.bfloat16)
    return np.stack([high, low])


def twist_columns():
    phase = 2.0 * np.pi * np.outer(np.arange(INNER), np.arange(1, KEPT)) / (RADIX * INNER)
    columns = np.zeros((INNER, LANES), np.float32)
    columns[:, :HALF] = np.cos(phase)
    columns[:, HALF : 2 * HALF] = np.sin(phase)
    return columns


def cmul(a, c, s):
    return (a[0] * c - a[1] * s, a[0] * s + a[1] * c)


def cadd(a, b):
    return (a[0] + b[0], a[1] + b[1])


def csub(a, b):
    return (a[0] - b[0], a[1] - b[1])


def times_i(a):
    return (-a[1], a[0])


def spread(x):
    s = math.sqrt(0.5)
    a = [x[q] + x[q + 4] for q in range(4)]
    b = [x[q] - x[q + 4] for q in range(4)]
    out = [None] * KEPT
    out[0] = (a[0] + a[2]) + (a[1] + a[3])
    out[8] = (a[0] + a[2]) - (a[1] + a[3])
    out[4] = (a[0] - a[2], a[3] - a[1])
    diff, both = s * (b[1] - b[3]), s * (b[1] + b[3])
    out[2] = (b[0] + diff, -b[2] - both)
    out[6] = (b[0] - diff, b[2] - both)
    u = [(x[0], -x[4])]
    for q in range(1, 4):
        c, t = math.cos(2.0 * math.pi * q / RADIX), math.sin(2.0 * math.pi * q / RADIX)
        u.append((x[q] * c - x[q + 4] * t, -(x[q + 4] * c + x[q] * t)))
    e0, e1 = cadd(u[0], u[2]), csub(u[0], u[2])
    f0, f1 = cadd(u[1], u[3]), times_i(csub(u[1], u[3]))
    out[1] = cadd(e0, f0)
    out[5] = csub(e1, f1)
    v2, v3 = csub(e0, f0), cadd(e1, f1)
    out[7] = (v2[0], -v2[1])
    out[3] = (v3[0], -v3[1])
    return out


def gather(z):
    s = math.sqrt(0.5)
    total, diff = z[0] + z[8], z[0] - z[8]
    plus, minus = total + z[4][0], total - z[4][0]
    sr, si = z[2][0] + z[6][0], z[6][1] - z[2][1]
    p = (s * (z[2][0] - z[2][1]), s * (z[2][0] + z[2][1]))
    w = (-s * (z[6][0] + z[6][1]), s * (z[6][0] - z[6][1]))
    pw, wp = p[0] + w[0], w[1] - p[1]
    down, up = diff - z[4][1], diff + z[4][1]
    even = [plus + sr, down + pw, minus + si, up + wp, plus - sr, down - pw, minus - si, up - wp]
    v = [z[1], z[5], (z[7][0], -z[7][1]), (z[3][0], -z[3][1])]
    e0, e1 = cadd(v[0], v[2]), csub(v[0], v[2])
    f0, f1 = cadd(v[1], v[3]), times_i(csub(v[1], v[3]))
    u = [cadd(e0, f0), cadd(e1, f1), csub(e0, f0), csub(e1, f1)]
    out = [None] * HALF
    for q in range(4):
        o = cmul(u[q], math.cos(2.0 * math.pi * q / RADIX), math.sin(2.0 * math.pi * q / RADIX))
        out[q] = even[q] + o[0]
        out[q + 4] = even[q + 4] - o[1]
    return out


def put_parts(high_ref, low_ref, row, r, value):
    high = value.astype(jnp.bfloat16)
    at = (pl.ds(pl.multiple_of(row, ROWS), ROWS), pl.ds(r * LANES, LANES))
    high_ref[at] = high
    low_ref[at] = (value - high.astype(jnp.float32)).astype(jnp.bfloat16)


def inner_dft(table_ref, high_ref, low_ref, out_ref):
    def block(at):
        high, low = high_ref[:, at], low_ref[:, at]
        out_ref[:, at] = (
            jnp.dot(table_ref[0], high, preferred_element_type=jnp.float32)
            + jnp.dot(table_ref[0], low, preferred_element_type=jnp.float32)
            + jnp.dot(table_ref[1], high, preferred_element_type=jnp.float32)
        )

    @pl.loop(0, HALF // 2)
    def _(i):
        block(pl.ds(pl.multiple_of(i * 2 * LANES, 2 * LANES), 2 * LANES))

    block(pl.ds(HALF * LANES, LANES))


def transform(source_ref, twist_ref, table_ref, high_ref, low_ref, spec_ref):
    @pl.loop(0, INNER // ROWS)
    def _(i):
        row = i * ROWS
        rows = pl.ds(pl.multiple_of(row, ROWS), ROWS)
        x = [
            source_ref[pl.ds(pl.multiple_of(q * INNER + row, ROWS), ROWS), :].astype(jnp.float32)
            for q in range(HALF)
        ]
        out = spread(x)
        put_parts(high_ref, low_ref, row, 0, out[0])
        put_parts(high_ref, low_ref, INNER + row, 0, jnp.zeros_like(out[0]))
        out[8] = (out[8], None)
        for r in range(1, KEPT):
            c, s = twist_ref[r - 1, rows, :], twist_ref[HALF + r - 1, rows, :]
            re, im = out[r]
            if im is None:
                re, im = re * c, -(re * s)
            else:
                re, im = re * c + im * s, im * c - re * s
            put_parts(high_ref, low_ref, row, r, re)
            put_parts(high_ref, low_ref, INNER + row, r, im)

    inner_dft(table_ref, high_ref, low_ref, spec_ref)


def correlate(left_ref, right_ref, twist_ref, table_ref, high_ref, low_ref, work_ref, store, flush):
    @pl.loop(0, INNER // ROWS)
    def _(i):
        row = i * ROWS
        top = pl.ds(pl.multiple_of(row, ROWS), ROWS)
        bottom = pl.ds(pl.multiple_of(INNER + row, ROWS), ROWS)
        for r in range(KEPT):
            lanes = pl.ds(r * LANES, LANES)
            scale = (1.0 if r in (0, HALF) else 2.0) / (RADIX * INNER)
            lr, li = left_ref[top, lanes] * scale, left_ref[bottom, lanes] * scale
            rr, ri = right_ref[top, lanes], right_ref[bottom, lanes]
            put_parts(high_ref, low_ref, row, r, li * rr - lr * ri)
            put_parts(high_ref, low_ref, INNER + row, r, lr * rr + li * ri)

    inner_dft(table_ref, high_ref, low_ref, work_ref)

    def finish(i):
        row = i * ROWS
        top = pl.ds(pl.multiple_of(row, ROWS), ROWS)
        bottom = pl.ds(pl.multiple_of(INNER + row, ROWS), ROWS)
        z = [work_ref[bottom, pl.ds(0, LANES)]]
        for r in range(1, KEPT):
            lanes = pl.ds(r * LANES, LANES)
            im, re = work_ref[top, lanes], work_ref[bottom, lanes]
            c, s = twist_ref[r - 1, top, :], twist_ref[HALF + r - 1, top, :]
            z.append((re * c - im * s, re * s + im * c))
        z[8] = z[8][0]
        for q, value in enumerate(gather(z)):
            store(q * INNER + row, value)

    steps = INNER // ROWS // 2
    pl.loop(0, steps)(finish)
    flush(0)
    pl.loop(steps, 2 * steps)(finish)
    flush(1)


def kernel(
    groups,
    grad_ref,
    input_ref,
    taps_ref,
    table_hbm,
    columns_hbm,
    grad_input_ref,
    filter_grad_ref,
    grad_in,
    taps_in,
    input_in,
    grad_spec,
    taps_spec,
    input_spec,
    work,
    high,
    low,
    twist,
    back,
    partial,
    arrived,
    table_ref,
    columns_ref,
    table_sem,
    send_sem,
    recv_sem,
    own_sem,
    pair_send,
    pair_recv,
):
    tokens = grad_ref.shape[0]
    half = partial.shape[0] // 2
    me = lax.axis_index("ctx")
    group = lax.axis_index("dp")
    other = 1 - group

    table_copy = pltpu.make_async_copy(table_hbm, table_ref, table_sem.at[0])
    columns_copy = pltpu.make_async_copy(columns_hbm, columns_ref, table_sem.at[1])
    columns_copy.start()
    table_copy.start()

    barrier = pltpu.get_barrier_semaphore()

    @pl.loop(1, groups)
    def _(d):
        pl.semaphore_signal(
            barrier, inc=1, device_id=(group, lax.rem(me + d, groups)), device_id_type=MESH
        )

    pl.semaphore_signal(barrier, inc=1, device_id=(other, me), device_id_type=MESH)
    pl.semaphore_wait(barrier, groups)

    def rows_of(device):
        return pl.ds(pl.multiple_of(device * tokens, tokens), tokens)

    def lanes_of(device):
        return pl.ds(pl.multiple_of(device * LANES, LANES), LANES)

    outward = ((grad_ref, grad_in), (input_ref, input_in), (taps_ref, taps_in))

    def copy_out(a, peer, dest_rows, recv_at):
        source, landing = outward[a]
        return pltpu.make_async_remote_copy(
            src_ref=source.at[:, lanes_of(peer)],
            dst_ref=landing.at[rows_of(dest_rows), :],
            send_sem=send_sem.at[a, peer],
            recv_sem=recv_sem.at[a, recv_at],
            device_id=(group, peer),
            device_id_type=MESH,
        )

    def copy_back(peer, dest_lanes, recv_at):
        return pltpu.make_async_remote_copy(
            src_ref=back.at[rows_of(peer), :],
            dst_ref=grad_input_ref.at[:, lanes_of(dest_lanes)],
            send_sem=send_sem.at[3, peer],
            recv_sem=recv_sem.at[3, recv_at],
            device_id=(group, peer),
            device_id_type=MESH,
        )

    def own_out(a):
        source, landing = outward[a]
        return pltpu.make_async_copy(
            source.at[:, lanes_of(me)], landing.at[rows_of(me), :], own_sem.at[a]
        )

    def own_back():
        return pltpu.make_async_copy(
            back.at[rows_of(me), :], grad_input_ref.at[:, lanes_of(me)], own_sem.at[3]
        )

    def send(a):
        @pl.loop(1, groups)
        def _(d):
            peer = lax.rem(me + d, groups)
            if a > 0:
                copy_out(a - 1, peer, peer, peer).wait_send()
            copy_out(a, peer, me, me).start()

    for a in range(3):
        own_out(a).start()
    send(0)

    columns_copy.wait()
    for i in range(2 * HALF):
        twist[i] = jnp.broadcast_to(columns_ref[:, i : i + 1], (INNER, LANES))
    table_copy.wait()

    def wait_for(a):
        own_out(a).wait()

        @pl.loop(1, groups)
        def _(d):
            peer = lax.rem(me + d, groups)
            copy_out(a, peer, peer, peer).wait_recv()

    shared = (twist, table_ref, high, low)
    send(1)
    wait_for(0)
    transform(grad_in, *shared, grad_spec)
    send(2)
    wait_for(1)
    transform(input_in, *shared, input_spec)

    def store_partial(row, value):
        partial[pl.ds(pl.multiple_of(row, ROWS), ROWS), :] = value

    def pair_copy(part, q):
        rows = INNER // 2
        at = q * INNER + part * rows
        return pltpu.make_async_remote_copy(
            src_ref=partial.at[pl.ds(pl.multiple_of(other * half + at, rows), rows), :],
            dst_ref=arrived.at[pl.ds(at, rows), :],
            send_sem=pair_send.at[part, q],
            recv_sem=pair_recv.at[part, q],
            device_id=(other, me),
            device_id_type=MESH,
        )

    def flush_partial(part):
        for q in range(HALF // 2):
            pair_copy(part, q).start()

    correlate(grad_spec, input_spec, *shared, work, store_partial, flush_partial)
    wait_for(2)
    transform(taps_in, *shared, taps_spec)

    def store_back(row, value):
        back[pl.ds(pl.multiple_of(row, ROWS), ROWS), :] = value.astype(jnp.bfloat16)

    def flush_back(part):
        @pl.loop(0, groups // 2)
        def _(d):
            peer = lax.rem(me + 2 * d, groups) // 2 * 2 + part

            @pl.when(peer != me)
            def _():
                copy_back(peer, me, me).start()

            @pl.when(peer == me)
            def _():
                own_back().start()

    correlate(grad_spec, taps_spec, *shared, work, store_back, flush_back)

    for part in range(2):
        for q in range(HALF // 2):
            pair_copy(part, q).wait()

    for i in range(half // LANES):
        mine = partial[pl.ds(pl.multiple_of(group * half + i * LANES, LANES), LANES), :]
        filter_grad_ref[:, i * LANES : (i + 1) * LANES] = jnp.transpose(
            mine + arrived[i * LANES : (i + 1) * LANES, :]
        )

    own_back().wait()

    @pl.loop(1, groups)
    def _(d):
        peer = lax.rem(me + d, groups)
        copy_back(peer, peer, peer).wait()
        copy_out(2, peer, peer, peer).wait_send()


def fused(grad_output, conv_input, filter_taps):
    groups = lax.axis_size("ctx")
    tokens, width = filter_taps.shape
    length = groups * tokens
    anywhere = pl.BlockSpec(memory_space=pl.ANY)
    vmem = pl.BlockSpec(memory_space=pltpu.VMEM)
    landing = pltpu.VMEM((length, LANES), jnp.bfloat16)
    spec = pltpu.VMEM((2 * INNER, KEPT * LANES), jnp.float32)
    part = pltpu.VMEM((2 * INNER, KEPT * LANES), jnp.bfloat16)
    grad_input, filter_grad = pl.pallas_call(
        functools.partial(kernel, groups),
        out_shape=(
            jax.ShapeDtypeStruct((tokens, width), jnp.bfloat16),
            jax.ShapeDtypeStruct((LANES, length // 2), jnp.float32),
        ),
        in_specs=[anywhere] * 5,
        out_specs=(anywhere, vmem),
        scratch_shapes=[
            landing,
            landing,
            landing,
            spec,
            spec,
            spec,
            spec,
            part,
            part,
            pltpu.VMEM((2 * HALF, INNER, LANES), jnp.float32),
            pltpu.VMEM((length, LANES), jnp.bfloat16),
            pltpu.VMEM((length, LANES), jnp.float32),
            pltpu.VMEM((length // 2, LANES), jnp.float32),
            pltpu.VMEM((2, 2 * INNER, 2 * INNER), jnp.bfloat16),
            pltpu.VMEM((INNER, LANES), jnp.float32),
            pltpu.SemaphoreType.DMA((2,)),
            pltpu.SemaphoreType.DMA((4, groups)),
            pltpu.SemaphoreType.DMA((4, groups)),
            pltpu.SemaphoreType.DMA((4,)),
            pltpu.SemaphoreType.DMA((2, HALF // 2)),
            pltpu.SemaphoreType.DMA((2, HALF // 2)),
        ],
        compiler_params=pltpu.CompilerParams(
            collective_id=0, has_side_effects=True, vmem_limit_bytes=63 * 1024 * 1024
        ),
        cost_estimate=pl.CostEstimate(
            flops=5 * 3 * 2 * 512 * 512 * KEPT * LANES, bytes_accessed=6 << 20, transcendentals=0
        ),
    )(
        grad_output[0],
        conv_input[0],
        filter_taps,
        jnp.asarray(inner_tables()),
        jnp.asarray(twist_columns()),
    )
    return (grad_input[None], filter_grad)


def any_size(grad_output, conv_input, filter_taps):
    groups = lax.axis_size("ctx")
    tokens, width = filter_taps.shape
    fits = (
        lax.axis_size("dp") == 2
        and groups * tokens == HALF * INNER
        and width == groups * LANES
        and 2 * tokens == INNER
    )
    return (fused if fits else local)(grad_output, conv_input, filter_taps)


def solution(mesh):
    placed = (P("dp", "ctx", None), P("dp", "ctx", None), P("ctx", None))
    return jax.shard_map(
        any_size,
        mesh=mesh,
        in_specs=placed,
        out_specs=(P("dp", "ctx", None), P("ctx", "dp")),
        check_vma=False,
    )
```

```python
import functools
import math

import jax
import jax.numpy as jnp
import numpy as np
from jax import lax
from jax.experimental import pallas as pl
from jax.experimental.pallas import tpu as pltpu
from jax.sharding import PartitionSpec as P


def angle_table(rows, cols, period):
    product = (
        lax.broadcasted_iota(jnp.int32, (rows, cols), 0)
        * lax.broadcasted_iota(jnp.int32, (rows, cols), 1)
        % period
    )
    phase = product.astype(jnp.float32) * (2.0 * math.pi / period)
    return (jnp.cos(phase), jnp.sin(phase))


def forward(values):
    blocks = values.shape[-2]
    tokens = values.shape[-1]
    rows = 2 * blocks
    block_cos, block_sin = angle_table(rows, blocks, rows)
    twist_cos, twist_sin = angle_table(rows, tokens, rows * tokens)
    inner_cos, inner_sin = angle_table(tokens, tokens, tokens)
    block_table = jnp.stack([block_cos, -block_sin])
    first = jnp.einsum("...qj,prq->...prj", values, block_table, precision=lax.Precision.HIGHEST)
    first_re = first[..., 0, :, :]
    first_im = first[..., 1, :, :]
    turned = jnp.stack(
        [first_re * twist_cos + first_im * twist_sin, first_im * twist_cos - first_re * twist_sin],
        axis=-3,
    )
    inner_table = jnp.stack([jnp.stack([inner_cos, -inner_sin]), jnp.stack([inner_sin, inner_cos])])
    return jnp.einsum("...prj,pojm->...orm", turned, inner_table, precision=lax.Precision.HIGHEST)


def inverse(spectrum):
    rows = spectrum.shape[-2]
    tokens = spectrum.shape[-1]
    blocks = rows // 2
    block_cos, block_sin = angle_table(rows, blocks, rows)
    twist_cos, twist_sin = angle_table(rows, tokens, rows * tokens)
    inner_cos, inner_sin = angle_table(tokens, tokens, tokens)
    inner_table = jnp.stack([jnp.stack([inner_cos, inner_sin]), jnp.stack([-inner_sin, inner_cos])])
    back = jnp.einsum("...prm,pomj->...orj", spectrum, inner_table, precision=lax.Precision.HIGHEST)
    back_re = back[..., 0, :, :]
    back_im = back[..., 1, :, :]
    turned = jnp.stack(
        [back_re * twist_cos - back_im * twist_sin, back_im * twist_cos + back_re * twist_sin],
        axis=-3,
    )
    block_table = jnp.stack([block_cos, -block_sin])
    result = jnp.einsum("...prj,prq->...qj", turned, block_table, precision=lax.Precision.HIGHEST)
    return result / (rows * tokens)


def conj_product(left, right):
    left_re = left[:, 0]
    left_im = left[:, 1]
    right_re = right[:, 0]
    right_im = right[:, 1]
    return jnp.stack(
        [left_re * right_re + left_im * right_im, left_im * right_re - left_re * right_im], axis=1
    )


def local(grad_output, conv_input, filter_taps):
    tokens = grad_output.shape[1]
    width = grad_output.shape[2]
    groups = lax.axis_size("ctx")
    group_width = width // groups

    def to_groups(values):
        return jnp.transpose(values.reshape(tokens, groups, group_width), (1, 2, 0))[:, :, None, :]

    grad_cols, input_cols, taps_cols = (
        lax.all_to_all(to_groups(grad_output[0]), "ctx", split_axis=0, concat_axis=2, tiled=True),
        lax.all_to_all(to_groups(conv_input[0]), "ctx", split_axis=0, concat_axis=2, tiled=True),
        lax.all_to_all(to_groups(filter_taps), "ctx", split_axis=0, concat_axis=2, tiled=True),
    )
    filter_spec = forward(taps_cols[0].astype(jnp.float32))
    stacked = jnp.stack([grad_cols[0], input_cols[0]]).astype(jnp.float32)
    spectra = forward(stacked)
    grad_spec = spectra[0]
    input_spec = spectra[1]
    cross = conj_product(grad_spec, filter_spec)
    corr = conj_product(grad_spec, input_spec)
    results = inverse(jnp.stack([cross, corr]))
    grad_cols_out = results[0]
    filter_part = lax.psum_scatter(results[1], "dp", scatter_dimension=1, tiled=True)
    filter_grad = filter_part.reshape(group_width, -1)
    rounded = grad_cols_out.astype(jnp.bfloat16)[None]
    returned = lax.all_to_all(rounded, "ctx", split_axis=2, concat_axis=0, tiled=True)
    grad_input = jnp.transpose(returned[:, :, 0, :], (2, 0, 1)).reshape(tokens, width)[None]
    return (grad_input, filter_grad)


INNER = 256
RADIX = 16
HALF = RADIX // 2
KEPT = HALF + 1
LANES = 128
ROWS = 16
MESH = pl.DeviceIdType.MESH


def inner_tables():
    index = np.arange(INNER)
    phase = 2.0 * np.pi * (np.outer(index, index) % INNER) / INNER
    cos, sin = np.cos(phase), np.sin(phase)
    table = np.block([[cos, sin], [-sin, cos]]).astype(np.float32)
    table = table.reshape(2, 2, INNER // 2, 2 * INNER).transpose(1, 0, 2, 3).reshape(table.shape)
    high = table.astype(jnp.bfloat16)
    low = (table - high.astype(np.float32)).astype(jnp.bfloat16)
    return np.stack([high, low])


def twist_columns():
    phase = 2.0 * np.pi * np.outer(np.arange(INNER), np.arange(1, KEPT)) / (RADIX * INNER)
    columns = np.zeros((INNER, LANES), np.float32)
    columns[:, :HALF] = np.cos(phase)
    columns[:, HALF : 2 * HALF] = np.sin(phase)
    return columns


def cmul(a, c, s):
    return (a[0] * c - a[1] * s, a[0] * s + a[1] * c)


def cadd(a, b):
    return (a[0] + b[0], a[1] + b[1])


def csub(a, b):
    return (a[0] - b[0], a[1] - b[1])


def times_i(a):
    return (-a[1], a[0])


def spread(x):
    s = math.sqrt(0.5)
    a = [x[q] + x[q + 4] for q in range(4)]
    b = [x[q] - x[q + 4] for q in range(4)]
    out = [None] * KEPT
    out[0] = (a[0] + a[2]) + (a[1] + a[3])
    out[8] = (a[0] + a[2]) - (a[1] + a[3])
    out[4] = (a[0] - a[2], a[3] - a[1])
    diff, both = s * (b[1] - b[3]), s * (b[1] + b[3])
    out[2] = (b[0] + diff, -b[2] - both)
    out[6] = (b[0] - diff, b[2] - both)
    u = [(x[0], -x[4])]
    for q in range(1, 4):
        c, t = math.cos(2.0 * math.pi * q / RADIX), math.sin(2.0 * math.pi * q / RADIX)
        u.append((x[q] * c - x[q + 4] * t, -(x[q + 4] * c + x[q] * t)))
    e0, e1 = cadd(u[0], u[2]), csub(u[0], u[2])
    f0, f1 = cadd(u[1], u[3]), times_i(csub(u[1], u[3]))
    out[1] = cadd(e0, f0)
    out[5] = csub(e1, f1)
    v2, v3 = csub(e0, f0), cadd(e1, f1)
    out[7] = (v2[0], -v2[1])
    out[3] = (v3[0], -v3[1])
    return out


def gather(z):
    s = math.sqrt(0.5)
    total, diff = z[0] + z[8], z[0] - z[8]
    plus, minus = total + z[4][0], total - z[4][0]
    sr, si = z[2][0] + z[6][0], z[6][1] - z[2][1]
    p = (s * (z[2][0] - z[2][1]), s * (z[2][0] + z[2][1]))
    w = (-s * (z[6][0] + z[6][1]), s * (z[6][0] - z[6][1]))
    pw, wp = p[0] + w[0], w[1] - p[1]
    down, up = diff - z[4][1], diff + z[4][1]
    even = [plus + sr, down + pw, minus + si, up + wp, plus - sr, down - pw, minus - si, up - wp]
    v = [z[1], z[5], (z[7][0], -z[7][1]), (z[3][0], -z[3][1])]
    e0, e1 = cadd(v[0], v[2]), csub(v[0], v[2])
    f0, f1 = cadd(v[1], v[3]), times_i(csub(v[1], v[3]))
    u = [cadd(e0, f0), cadd(e1, f1), csub(e0, f0), csub(e1, f1)]
    out = [None] * HALF
    for q in range(4):
        o = cmul(u[q], math.cos(2.0 * math.pi * q / RADIX), math.sin(2.0 * math.pi * q / RADIX))
        out[q] = even[q] + o[0]
        out[q + 4] = even[q + 4] - o[1]
    return out


def put_parts(high_ref, low_ref, row, r, value):
    high = value.astype(jnp.bfloat16)
    at = (pl.ds(pl.multiple_of(row, ROWS), ROWS), pl.ds(r * LANES, LANES))
    high_ref[at] = high
    low_ref[at] = (value - high.astype(jnp.float32)).astype(jnp.bfloat16)


def inner_dft(table_ref, high_ref, low_ref, out_ref, rows):
    def block(at):
        high, low = high_ref[:, at], low_ref[:, at]
        out_ref[rows, at] = (
            jnp.dot(table_ref[0, rows, :], high, preferred_element_type=jnp.float32)
            + jnp.dot(table_ref[0, rows, :], low, preferred_element_type=jnp.float32)
            + jnp.dot(table_ref[1, rows, :], high, preferred_element_type=jnp.float32)
        )

    @pl.loop(0, HALF // 2)
    def _(i):
        block(pl.ds(pl.multiple_of(i * 2 * LANES, 2 * LANES), 2 * LANES))

    block(pl.ds(HALF * LANES, LANES))


def transform(source_ref, twist_ref, table_ref, high_ref, low_ref, spec_ref):
    @pl.loop(0, INNER // ROWS)
    def _(i):
        row = i * ROWS
        rows = pl.ds(pl.multiple_of(row, ROWS), ROWS)
        x = [
            source_ref[pl.ds(pl.multiple_of(q * INNER + row, ROWS), ROWS), :].astype(jnp.float32)
            for q in range(HALF)
        ]
        out = spread(x)
        put_parts(high_ref, low_ref, row, 0, out[0])
        put_parts(high_ref, low_ref, INNER + row, 0, jnp.zeros_like(out[0]))
        out[8] = (out[8], None)
        for r in range(1, KEPT):
            c, s = twist_ref[r - 1, rows, :], twist_ref[HALF + r - 1, rows, :]
            re, im = out[r]
            if im is None:
                re, im = re * c, -(re * s)
            else:
                re, im = re * c + im * s, im * c - re * s
            put_parts(high_ref, low_ref, row, r, re)
            put_parts(high_ref, low_ref, INNER + row, r, im)

    inner_dft(table_ref, high_ref, low_ref, spec_ref, pl.ds(0, 2 * INNER))


def correlate(left_ref, right_ref, twist_ref, table_ref, high_ref, low_ref, work_ref, store, flush):
    steps = INNER // ROWS // 2

    def parts(part, i):
        top = part * INNER + i * ROWS
        return (
            pl.ds(pl.multiple_of(top, ROWS), ROWS),
            pl.ds(pl.multiple_of(top + INNER // 2, ROWS), ROWS),
        )

    for part in range(2):

        @pl.loop(0, steps)
        def _(i):
            row = part * (INNER // 2) + i * ROWS
            top, bottom = parts(part, i)
            for r in range(KEPT):
                lanes = pl.ds(r * LANES, LANES)
                scale = (1.0 if r in (0, HALF) else 2.0) / (RADIX * INNER)
                lr, li = left_ref[top, lanes] * scale, left_ref[bottom, lanes] * scale
                rr, ri = right_ref[top, lanes], right_ref[bottom, lanes]
                put_parts(high_ref, low_ref, row, r, li * rr - lr * ri)
                put_parts(high_ref, low_ref, INNER + row, r, lr * rr + li * ri)

    for part in range(2):
        inner_dft(table_ref, high_ref, low_ref, work_ref, pl.ds(part * INNER, INNER))

        @pl.loop(0, steps)
        def _(i):
            row = part * (INNER // 2) + i * ROWS
            rows = pl.ds(pl.multiple_of(row, ROWS), ROWS)
            top, bottom = parts(part, i)
            z = [work_ref[bottom, pl.ds(0, LANES)]]
            for r in range(1, KEPT):
                lanes = pl.ds(r * LANES, LANES)
                im, re = work_ref[top, lanes], work_ref[bottom, lanes]
                c, s = twist_ref[r - 1, rows, :], twist_ref[HALF + r - 1, rows, :]
                z.append((re * c - im * s, re * s + im * c))
            z[8] = z[8][0]
            for q, value in enumerate(gather(z)):
                store(q * INNER + row, value)

        flush(part)


def kernel(
    groups,
    grad_ref,
    input_ref,
    taps_ref,
    table_hbm,
    columns_hbm,
    grad_input_ref,
    filter_grad_ref,
    grad_in,
    taps_in,
    input_in,
    grad_spec,
    taps_spec,
    input_spec,
    work,
    high,
    low,
    twist,
    back,
    partial,
    arrived,
    table_ref,
    columns_ref,
    table_sem,
    send_sem,
    recv_sem,
    own_sem,
    pair_send,
    pair_recv,
):
    tokens = grad_ref.shape[0]
    half = partial.shape[0] // 2
    me = lax.axis_index("ctx")
    group = lax.axis_index("dp")
    other = 1 - group

    table_copy = pltpu.make_async_copy(table_hbm, table_ref, table_sem.at[0])
    columns_copy = pltpu.make_async_copy(columns_hbm, columns_ref, table_sem.at[1])
    columns_copy.start()
    table_copy.start()

    barrier = pltpu.get_barrier_semaphore()

    @pl.loop(1, groups)
    def _(d):
        pl.semaphore_signal(
            barrier, inc=1, device_id=(group, lax.rem(me + d, groups)), device_id_type=MESH
        )

    pl.semaphore_signal(barrier, inc=1, device_id=(other, me), device_id_type=MESH)
    pl.semaphore_wait(barrier, groups)

    def rows_of(device):
        return pl.ds(pl.multiple_of(device * tokens, tokens), tokens)

    def lanes_of(device):
        return pl.ds(pl.multiple_of(device * LANES, LANES), LANES)

    outward = ((grad_ref, grad_in), (input_ref, input_in), (taps_ref, taps_in))

    def copy_out(a, peer, dest_rows, recv_at):
        source, landing = outward[a]
        return pltpu.make_async_remote_copy(
            src_ref=source.at[:, lanes_of(peer)],
            dst_ref=landing.at[rows_of(dest_rows), :],
            send_sem=send_sem.at[a, peer],
            recv_sem=recv_sem.at[a, recv_at],
            device_id=(group, peer),
            device_id_type=MESH,
        )

    def copy_back(peer, dest_lanes, recv_at):
        return pltpu.make_async_remote_copy(
            src_ref=back.at[rows_of(peer), :],
            dst_ref=grad_input_ref.at[:, lanes_of(dest_lanes)],
            send_sem=send_sem.at[3, peer],
            recv_sem=recv_sem.at[3, recv_at],
            device_id=(group, peer),
            device_id_type=MESH,
        )

    def own_out(a):
        source, landing = outward[a]
        return pltpu.make_async_copy(
            source.at[:, lanes_of(me)], landing.at[rows_of(me), :], own_sem.at[a]
        )

    def own_back():
        return pltpu.make_async_copy(
            back.at[rows_of(me), :], grad_input_ref.at[:, lanes_of(me)], own_sem.at[3]
        )

    for a in range(3):

        @pl.loop(1, groups)
        def _(d):
            copy_out(a, lax.rem(me + d, groups), me, me).start()

        own_out(a).start()

    columns_copy.wait()
    for i in range(2 * HALF):
        twist[i] = jnp.broadcast_to(columns_ref[:, i : i + 1], (INNER, LANES))
    table_copy.wait()

    def wait_for(a):
        own_out(a).wait()

        @pl.loop(1, groups)
        def _(d):
            peer = lax.rem(me + d, groups)
            copy_out(a, peer, peer, peer).wait_recv()

    shared = (twist, table_ref, high, low)
    wait_for(0)
    transform(grad_in, *shared, grad_spec)
    wait_for(1)
    transform(input_in, *shared, input_spec)

    def store_partial(row, value):
        partial[pl.ds(pl.multiple_of(row, ROWS), ROWS), :] = value

    def pair_copy(part, q):
        rows = INNER // 2
        at = q * INNER + part * rows
        return pltpu.make_async_remote_copy(
            src_ref=partial.at[pl.ds(pl.multiple_of(other * half + at, rows), rows), :],
            dst_ref=arrived.at[pl.ds(at, rows), :],
            send_sem=pair_send.at[part, q],
            recv_sem=pair_recv.at[part, q],
            device_id=(other, me),
            device_id_type=MESH,
        )

    def flush_partial(part):
        for q in range(HALF // 2):
            pair_copy(part, q).start()

    correlate(grad_spec, input_spec, *shared, work, store_partial, flush_partial)
    wait_for(2)
    transform(taps_in, *shared, taps_spec)

    def store_back(row, value):
        back[pl.ds(pl.multiple_of(row, ROWS), ROWS), :] = value.astype(jnp.bfloat16)

    def flush_back(part):
        @pl.loop(0, groups // 2)
        def _(d):
            peer = lax.rem(me + 2 * d, groups) // 2 * 2 + part

            @pl.when(peer != me)
            def _():
                copy_back(peer, me, me).start()

            @pl.when(peer == me)
            def _():
                own_back().start()

    correlate(grad_spec, taps_spec, *shared, work, store_back, flush_back)

    for part in range(2):
        for q in range(HALF // 2):
            pair_copy(part, q).wait()

    for i in range(half // LANES):
        mine = partial[pl.ds(pl.multiple_of(group * half + i * LANES, LANES), LANES), :]
        filter_grad_ref[i * LANES : (i + 1) * LANES, :] = (
            mine + arrived[i * LANES : (i + 1) * LANES, :]
        )

    own_back().wait()

    @pl.loop(1, groups)
    def _(d):
        peer = lax.rem(me + d, groups)
        copy_back(peer, peer, peer).wait()
        for a in range(3):
            copy_out(a, peer, peer, peer).wait_send()


def fused(grad_output, conv_input, filter_taps):
    groups = lax.axis_size("ctx")
    tokens, width = filter_taps.shape
    length = groups * tokens
    anywhere = pl.BlockSpec(memory_space=pl.ANY)
    vmem = pl.BlockSpec(memory_space=pltpu.VMEM)
    landing = pltpu.VMEM((length, LANES), jnp.bfloat16)
    spec = pltpu.VMEM((2 * INNER, KEPT * LANES), jnp.float32)
    part = pltpu.VMEM((2 * INNER, KEPT * LANES), jnp.bfloat16)
    grad_input, filter_grad = pl.pallas_call(
        functools.partial(kernel, groups),
        out_shape=(
            jax.ShapeDtypeStruct((tokens, width), jnp.bfloat16),
            jax.ShapeDtypeStruct((length // 2, LANES), jnp.float32),
        ),
        in_specs=[anywhere] * 5,
        out_specs=(anywhere, vmem),
        scratch_shapes=[
            landing,
            landing,
            landing,
            spec,
            spec,
            spec,
            spec,
            part,
            part,
            pltpu.VMEM((2 * HALF, INNER, LANES), jnp.float32),
            pltpu.VMEM((length, LANES), jnp.bfloat16),
            pltpu.VMEM((length, LANES), jnp.float32),
            pltpu.VMEM((length // 2, LANES), jnp.float32),
            pltpu.VMEM((2, 2 * INNER, 2 * INNER), jnp.bfloat16),
            pltpu.VMEM((INNER, LANES), jnp.float32),
            pltpu.SemaphoreType.DMA((2,)),
            pltpu.SemaphoreType.DMA((4, groups)),
            pltpu.SemaphoreType.DMA((4, groups)),
            pltpu.SemaphoreType.DMA((4,)),
            pltpu.SemaphoreType.DMA((2, HALF // 2)),
            pltpu.SemaphoreType.DMA((2, HALF // 2)),
        ],
        compiler_params=pltpu.CompilerParams(
            collective_id=0, has_side_effects=True, vmem_limit_bytes=63 * 1024 * 1024
        ),
        cost_estimate=pl.CostEstimate(
            flops=5 * 3 * 2 * 512 * 512 * KEPT * LANES, bytes_accessed=6 << 20, transcendentals=0
        ),
    )(
        grad_output[0],
        conv_input[0],
        filter_taps,
        jnp.asarray(inner_tables()),
        jnp.asarray(twist_columns()),
    )
    return (grad_input[None], jnp.transpose(filter_grad))


def any_size(grad_output, conv_input, filter_taps):
    groups = lax.axis_size("ctx")
    tokens, width = filter_taps.shape
    fits = (
        lax.axis_size("dp") == 2
        and groups * tokens == HALF * INNER
        and width == groups * LANES
        and 2 * tokens == INNER
    )
    return (fused if fits else local)(grad_output, conv_input, filter_taps)


def solution(mesh):
    placed = (P("dp", "ctx", None), P("dp", "ctx", None), P("ctx", None))
    return jax.shard_map(
        any_size,
        mesh=mesh,
        in_specs=placed,
        out_specs=(P("dp", "ctx", None), P("ctx", "dp")),
        check_vma=False,
    )
```
